32 devices in a mesh: groups: 1, ep: 32 (over z, y, x, core).
Axes of the slice: x: 2, y: 2, z: 4, core: 2. Of those that a mesh axis runs over, the one named last changes fastest.
Arguments:
- kv_cache: bfloat16 [256, 32, 512], P(('groups', 'ep')), may hold values from -4.5 to 4.5
- cache_length: int32 [256], P(('groups', 'ep')), may hold values from 2 to 32, as said below
- dest_device: int32 [256], P(('groups', 'ep')), may hold values from 0 to 31, as said below
- dest_slot: int32 [256], P(('groups', 'ep')), may hold values from 0 to 7, as said below
- query_rows: bfloat16 [256, 4096], P(('groups', 'ep')), may hold values from -4.5 to 4.5
- new_kv: bfloat16 [256, 512], P(('groups', 'ep')), may hold values from -4.5 to 4.5
- resid_rows: bfloat16 [256, 4096], P(('groups', 'ep')), may hold values from -3 to 3
- norm_gain: bfloat16 [4096], replicated, may hold values from 0.099609375 to 1.8984375
- route_ids: int32 [256, 8], P(('groups', 'ep')), may hold values from 0 to 15, all different within a row; in each aligned block of 8 rows (0 to 7, 8 to 15, ...) at most 8 rows name the same one
- route_weight: bfloat16 [256, 8], P(('groups', 'ep')), may hold values from 0.049804688 to 0.3984375
- w_gate: bfloat16 [32, 4096, 384], P('ep'), may hold values from -0.09375 to 0.09375
- w_up: bfloat16 [32, 4096, 384], P('ep'), may hold values from -0.09375 to 0.09375
- w_down: bfloat16 [32, 384, 4096], P('ep'), may hold values from -0.21875 to 0.21875
Outputs:
- moved_cache: bfloat16 [256, 32, 512], P(('groups', 'ep'))
- context: bfloat16 [256, 4096], P(('groups', 'ep'))
- moe_out: bfloat16 [256, 4096], P(('groups', 'ep'))
The draws below stay inside these ranges and needn't reach their ends.
Inputs may be any that keep to these rules, and one draw needn't show every extreme that they name: `dest_device`: device d hands exactly 2 of its requests to each of the devices d, d + 1, ..., d + 3 along ep (indices modulo the number of devices), so every device receives exactly 8 requests. `dest_slot`: the requests that arrive at one device take distinct slots. `cache_length`: every device holds a request of length exactly 32. `route_ids`: the 8 experts of a row differ; among the rows of one device no expert is named by more than 8 rows.
All inputs are finite; a program needn't handle non-finite values.
Results may differ from the reference program's by a relative error of at most 0.014.
Values may be sent and summed in bfloat16 or wider, within the bound.
A program may use at most 64 MiB of HBM per device.

```python
import math
import jax
import jax.numpy as jnp
import numpy as np
from jax import lax

D = 4096
HEAD_DIM = 128
Q_HEADS = 32
KV_HEADS = 2
FF = 768
TOPK = 8
SPAN = 4
REQ_DEV = 8
LEN = 32
REQUESTS = 256
EXPERTS = 16
CAP = 8
N_EP = 32


def plan_tables(key):
    device_count = REQUESTS // REQ_DEV
    slot_ids = jnp.arange(REQ_DEV)
    first_score = jax.random.randint(jax.random.fold_in(key, 11), (device_count, REQ_DEV), 0, 1 << 20) * REQ_DEV + slot_ids[None, :]
    second_score = jax.random.randint(jax.random.fold_in(key, 12), (device_count, REQ_DEV), 0, 1 << 20) * REQ_DEV + slot_ids[None, :]
    position = jnp.argsort(jnp.argsort(first_score, axis=1), axis=1)
    seats = jnp.argsort(jnp.argsort(second_score, axis=1), axis=1)
    offset = position // (REQ_DEV // SPAN)
    target = (jnp.arange(device_count)[:, None] + offset) % device_count
    slots = seats[target, position]
    return (target.reshape(-1).astype(jnp.int32), slots.reshape(-1).astype(jnp.int32))


def draw_dest_device(key, part):
    shared = plan_tables(key)
    return shared[0]


def draw_dest_slot(key, part):
    shared = plan_tables(key)
    return shared[1]


def draw_cache_length(key, part):
    key = jax.random.fold_in(key, 3)
    device_count = REQUESTS // REQ_DEV
    first_draw = jax.random.randint(jax.random.fold_in(key, 1), (device_count, REQ_DEV), 2, LEN + 1)
    second_draw = jax.random.randint(jax.random.fold_in(key, 2), (device_count, REQ_DEV), 2, LEN + 1)
    longest = jax.random.randint(jax.random.fold_in(key, 3), (device_count, 1), 0, REQ_DEV)
    lengths = jnp.where(jnp.arange(REQ_DEV)[None, :] == longest, LEN, jnp.minimum(first_draw, second_draw))
    return lengths.reshape(-1).astype(jnp.int32)


def draw_kv_cache(key, part):
    key = jax.random.fold_in(key, 4)
    shape = (REQUESTS, LEN, 2, KV_HEADS, HEAD_DIM)
    values = jnp.clip(jax.random.normal(jax.random.fold_in(key, 1), shape, jnp.float32), -4.5, 4.5)
    return values.reshape(REQUESTS, LEN, 2 * KV_HEADS * HEAD_DIM).astype(jnp.bfloat16)


def draw_query_rows(key, part):
    key = jax.random.fold_in(key, 5)
    group_size = Q_HEADS // KV_HEADS
    shape = (REQUESTS, KV_HEADS, group_size, HEAD_DIM)
    values = jnp.clip(jax.random.normal(jax.random.fold_in(key, 1), shape, jnp.float32), -4.5, 4.5)
    return values.reshape(REQUESTS, Q_HEADS * HEAD_DIM).astype(jnp.bfloat16)


def block_levels(own_key, dims, split, low, largest):
    factor_of = 1.0
    for dim, parts in split:
        steps = jax.random.uniform(jax.random.fold_in(jax.random.fold_in(own_key, 6), dim), (parts,), jnp.float32, low / len(split), largest / len(split))
        factor_of = factor_of * jnp.repeat(jnp.exp(steps), dims[dim] // parts).reshape((-1,) + (1,) * (len(dims) - 1 - dim))
    return factor_of


def routed_block(rng, own, number, rows, amount, top, bound, slope):
    sequence = jax.random.permutation(rng, amount)
    crowded, common = shares(amount, rows * top, bound, slope, True), shares(amount, rows * top, bound, slope, False)
    places = jnp.arange(amount)

    def named(sizes, offset_by):
        used = int((sizes > 0).sum())
        fixed = max(1, used // 4)
        moved = fixed + (places - fixed + offset_by * (used - fixed)) % max(1, amount - fixed)
        return jnp.zeros((amount,), jnp.int32).at[sequence[jnp.where(places < fixed, places, moved)]].set(jnp.asarray(sizes, jnp.int32))

    sizes = jnp.where(number % 4 == 0, named(crowded, number // 4), named(common, number - number // 4 - 1))
    mixed = jax.random.permutation(jax.random.fold_in(own, 3), amount)
    source_of, receiver = mixed[0:amount // 2 * 2:2], mixed[1:amount // 2 * 2:2]
    margin = jnp.minimum(sizes[source_of] - 1, bound - sizes[receiver]) // 2
    margin = jnp.where((source_of == sequence[0]) | (receiver == sequence[0]) | (sizes[receiver] == 0), 0, jnp.maximum(margin, 0))
    moved = jax.random.randint(jax.random.fold_in(own, 4), (amount // 2,), 0, 1 << 20) % (margin + 1)
    sizes = sizes.at[source_of].add(-moved).at[receiver].add(moved)
    items = jnp.searchsorted(jnp.cumsum(sizes), jnp.arange(rows * top), side="right").astype(jnp.int32)
    grid = items.reshape(top, rows).T
    grid = grid[jax.random.permutation(jax.random.fold_in(own, 1), rows)]
    offset_by = jax.random.randint(jax.random.fold_in(own, 2), (rows, 1), 0, top)
    return jnp.take_along_axis(grid, (jnp.arange(top)[None, :] + offset_by) % top, axis=1)


def shares(count, total, reach, slope, full):
    portions = [(1 << 20) // math.isqrt(grade ** slope) + 1 for grade in range(1, count + 1)]
    largest = reach if full else min(reach, max(-(-total // count), total * portions[0] // sum(portions)))
    least = 1 if total - largest >= count - 1 else 0
    given, surplus = [largest] + [least] * (count - 1), total - largest - least * (count - 1)
    while surplus > 0:
        candidates = [i for i in range(1, count) if given[i] < largest] or [i for i in range(1, count) if given[i] < reach]
        pool, budget = sum([portions[i] for i in candidates]), surplus
        for i in candidates:
            more = min(reach - given[i], max(1, budget * portions[i] // pool), surplus)
            given[i] = given[i] + more
            surplus = surplus - more
    return np.array(given)


def gaussian(rng, extent, scale, most, shards=(), kind=jnp.bfloat16):
    gain = block_levels(rng, extent, shards, -0.22, 0.18) if shards else 1.0
    drawn = jax.random.normal(rng, extent, jnp.float32) * scale * gain
    return jnp.minimum(jnp.maximum(drawn, -most), most).astype(kind)


def setup_inputs(seed: int = 0, part: int = 0) -> dict:
    seeds = jax.random.split(jax.random.key(seed), 14)
    part_splits = jax.random.split(jax.random.fold_in(seeds[13], part), 14)
    kv_cache = draw_kv_cache(jax.random.fold_in(jax.random.fold_in(seeds[13], part), 71), part)
    cache_length = draw_cache_length(jax.random.fold_in(jax.random.fold_in(seeds[13], part), 71), part)
    dest_device = draw_dest_device(jax.random.fold_in(jax.random.fold_in(seeds[13], part), 71), part)
    dest_slot = draw_dest_slot(jax.random.fold_in(jax.random.fold_in(seeds[13], part), 71), part)
    query_rows = draw_query_rows(jax.random.fold_in(jax.random.fold_in(seeds[13], part), 71), part)
    new_kv = gaussian(part_splits[5], (REQUESTS, 2 * KV_HEADS * HEAD_DIM), 1.0, 4.5, ((0, 32),))
    resid_rows = gaussian(part_splits[6], (REQUESTS, D), 0.5, 3.0, ((0, 32),))
    norm_gain = jnp.clip(1.0 + 0.18 * jax.random.normal(seeds[7], (D,), jnp.float32), 0.099609375, 1.8984375).astype(jnp.bfloat16)
    route_ids_keys = jax.random.split(jax.random.fold_in(part_splits[8], 1), REQUESTS // REQ_DEV)
    route_ids_turns = jax.random.permutation(jax.random.fold_in(part_splits[8], 3), REQUESTS // REQ_DEV)
    route_ids = jax.vmap(lambda own, number: routed_block(jax.random.fold_in(part_splits[8], 2), own, number, REQ_DEV, EXPERTS, TOPK, CAP, 2))(route_ids_keys, route_ids_turns).reshape((REQUESTS, TOPK))
    route_weight = jnp.clip(jnp.exp(math.log(0.3984375) - 2.0794415 * jax.random.uniform(part_splits[9], (REQUESTS, TOPK), jnp.float32) ** block_levels(part_splits[9], (REQUESTS, TOPK), ((0, 32),), -0.2, 0.2)), 0.049804688, 0.3984375).astype(jnp.bfloat16)
    w_gate = gaussian(seeds[10], (2 * EXPERTS, D, FF // 2), D ** -0.5, 0.09375, ((0, 32),))
    w_up = gaussian(seeds[11], (2 * EXPERTS, D, FF // 2), D ** -0.5, 0.09375, ((0, 32),))
    w_down = gaussian(seeds[12], (2 * EXPERTS, FF // 2, D), FF ** -0.5, 0.21875, ((0, 32),))
    return {"kv_cache": kv_cache, "cache_length": cache_length, "dest_device": dest_device, "dest_slot": dest_slot, "query_rows": query_rows, "new_kv": new_kv, "resid_rows": resid_rows, "norm_gain": norm_gain, "route_ids": route_ids, "route_weight": route_weight, "w_gate": w_gate, "w_up": w_up, "w_down": w_down}


def attend(query_rows, new_kv, kv_cache, cache_length):
    row_count = query_rows.shape[0]
    group_size = Q_HEADS // KV_HEADS
    score_scale = 1.0 / math.sqrt(HEAD_DIM)
    queries = query_rows.reshape(row_count, KV_HEADS, group_size, HEAD_DIM).astype(jnp.float32)
    stored = kv_cache.reshape(row_count, LEN, 2, KV_HEADS, HEAD_DIM).astype(jnp.float32)
    fresh = new_kv.reshape(row_count, 2, KV_HEADS, HEAD_DIM).astype(jnp.float32)
    scores = jnp.einsum('rgjd,rtgd->rgjt', queries, stored[:, :, 0]) * score_scale
    own_score = jnp.einsum('rgjd,rgd->rgj', queries, fresh[:, 0]) * score_scale
    in_range = (jnp.arange(LEN, dtype=jnp.int32)[None, :] < cache_length[:, None])[:, None, None, :]
    masked = jnp.where(in_range, scores, -jnp.inf)
    peak = jnp.maximum(lax.optimization_barrier(jnp.max(masked, axis=-1)), own_score)
    weights = jnp.where(in_range, jnp.exp(scores - peak[..., None]), 0.0)
    own_weight = jnp.exp(own_score - peak)
    denominator = lax.optimization_barrier(jnp.sum(weights, axis=-1)) + own_weight
    probs = (weights / denominator[..., None]).astype(jnp.bfloat16)
    own_prob = (own_weight / denominator).astype(jnp.bfloat16)
    context = jnp.einsum('rgjt,rtgd->rgjd', probs.astype(jnp.float32), stored[:, :, 1])
    context = context + own_prob.astype(jnp.float32)[..., None] * fresh[:, 1][:, :, None, :]
    return context.reshape(row_count, Q_HEADS * HEAD_DIM).astype(jnp.bfloat16)

def expert_half(row_block, gate_matrix, up_matrix, down_matrix):
    gate_part = jnp.dot(row_block, gate_matrix, preferred_element_type=jnp.float32)
    up_part = jnp.dot(row_block, up_matrix, preferred_element_type=jnp.float32)
    hidden = (jax.nn.silu(gate_part) * up_part).astype(jnp.bfloat16)
    return jnp.dot(hidden, down_matrix, preferred_element_type=jnp.float32).astype(jnp.bfloat16)

def slot_numbers(route_ids):
    flat_ids = route_ids.reshape(-1, REQ_DEV * TOPK)
    onehot = (flat_ids[:, :, None] == jnp.arange(EXPERTS, dtype=jnp.int32)[None, None, :]).astype(jnp.int32)
    before = jnp.cumsum(onehot, axis=1) - onehot
    return lax.optimization_barrier(jnp.sum(before * onehot, axis=2)).reshape(-1, TOPK).astype(jnp.int32)

def reference(kv_cache, cache_length, dest_device, dest_slot, query_rows, new_kv, resid_rows, norm_gain, route_ids, route_weight, w_gate, w_up, w_down):
    target = (dest_device * REQ_DEV + dest_slot).astype(jnp.int32)
    moved_cache = jnp.zeros_like(kv_cache).at[target].set(kv_cache)
    moved_length = jnp.zeros_like(cache_length).at[target].set(cache_length)
    context = attend(query_rows, new_kv, moved_cache, moved_length)
    summed_state = resid_rows.astype(jnp.float32) + context.astype(jnp.float32)
    inverse = lax.rsqrt(lax.optimization_barrier(jnp.mean(summed_state * summed_state, axis=1, keepdims=True)) + 1e-06)
    normed = (summed_state * inverse * norm_gain.astype(jnp.float32)[None, :]).astype(jnp.bfloat16)
    slot_index = slot_numbers(route_ids)
    row_ids = jnp.arange(REQUESTS, dtype=jnp.int32)
    blocks = (row_ids // REQ_DEV).astype(jnp.int32)
    row_table = jnp.full((EXPERTS, N_EP, CAP), REQUESTS, jnp.int32)
    row_table = row_table.at[route_ids, blocks[:, None], slot_index].set(jnp.broadcast_to(row_ids[:, None], route_ids.shape))
    padded = jnp.concatenate([normed, jnp.zeros((1, D), jnp.bfloat16)], axis=0)

    def run_expert(expert_index):
        row_block = padded[row_table[expert_index].reshape(-1)]
        lower_half = expert_half(row_block, w_gate[2 * expert_index], w_up[2 * expert_index], w_down[2 * expert_index])
        upper_half = expert_half(row_block, w_gate[2 * expert_index + 1], w_up[2 * expert_index + 1], w_down[2 * expert_index + 1])
        return (lower_half.astype(jnp.float32) + upper_half.astype(jnp.float32)).astype(jnp.bfloat16)
    expert_out = lax.map(run_expert, jnp.arange(EXPERTS, dtype=jnp.int32))
    combined = jnp.zeros((REQUESTS, D), jnp.float32)
    for column in range(TOPK):
        picked = expert_out[route_ids[:, column], blocks * CAP + slot_index[:, column]]
        combined = combined + route_weight[:, column].astype(jnp.float32)[:, None] * picked.astype(jnp.float32)
    return (moved_cache, context, combined.astype(jnp.bfloat16))
```

```python
import math

import jax
import jax.numpy as jnp
from jax import lax
from jax.sharding import PartitionSpec as P

HEAD_DIM = 128
Q_HEADS = 32
KV_HEADS = 2
TOPK = 8
SPAN = 4
LEN = 32


def from_behind(array, axis, by):
    peers = lax.axis_size(axis)
    return lax.ppermute(array, axis, [(i, (i + by) % peers) for i in range(peers)])


def attend(query_rows, new_kv, kv_cache, cache_length):
    row_count = query_rows.shape[0]
    group_size = Q_HEADS // KV_HEADS
    score_scale = 1.0 / math.sqrt(HEAD_DIM)
    queries = query_rows.reshape(row_count, KV_HEADS, group_size, HEAD_DIM)
    stored = kv_cache.reshape(row_count, LEN, 2, KV_HEADS, HEAD_DIM)
    fresh = new_kv.reshape(row_count, 2, KV_HEADS, HEAD_DIM)
    scores = (
        jnp.einsum("rgjd,rtgd->rgjt", queries, stored[:, :, 0], preferred_element_type=jnp.float32)
        * score_scale
    )
    own_score = (
        jnp.einsum("rgjd,rgd->rgj", queries, fresh[:, 0], preferred_element_type=jnp.float32)
        * score_scale
    )
    in_range = (jnp.arange(LEN, dtype=jnp.int32)[None, :] < cache_length[:, None])[:, None, None, :]
    masked = jnp.where(in_range, scores, -jnp.inf)
    peak = jnp.maximum(jnp.max(masked, axis=-1), own_score)
    weights = jnp.where(in_range, jnp.exp(scores - peak[..., None]), 0.0)
    own_weight = jnp.exp(own_score - peak)
    denominator = jnp.sum(weights, axis=-1) + own_weight
    probs = (weights / denominator[..., None]).astype(jnp.bfloat16)
    own_prob = (own_weight / denominator).astype(jnp.bfloat16)
    context = jnp.einsum(
        "rgjt,rtgd->rgjd", probs, stored[:, :, 1], preferred_element_type=jnp.float32
    )
    context = (
        context
        + own_prob.astype(jnp.float32)[..., None] * fresh[:, 1].astype(jnp.float32)[:, :, None, :]
    )
    return context.reshape(row_count, Q_HEADS * HEAD_DIM).astype(jnp.bfloat16)


def expert_half(row_block, gate_matrix, up_matrix, down_matrix):
    gate_part = jnp.dot(row_block, gate_matrix, preferred_element_type=jnp.float32)
    up_part = jnp.dot(row_block, up_matrix, preferred_element_type=jnp.float32)
    hidden = (jax.nn.silu(gate_part) * up_part).astype(jnp.bfloat16)
    return jnp.dot(hidden, down_matrix, preferred_element_type=jnp.float32)


def order_matrix(dest_device, device_count, owned_count, group_rows):
    offset = (dest_device - lax.axis_index("ep")) % device_count
    onehot = (offset[:, None] == jnp.arange(SPAN, dtype=jnp.int32)[None, :]).astype(jnp.int32)
    rank = jnp.sum((jnp.cumsum(onehot, axis=0) - onehot) * onehot, axis=1)
    position = offset * group_rows + rank
    return jnp.arange(owned_count, dtype=jnp.int32)[:, None] == position[None, :]


def apply_rows(selector, values):
    return jnp.dot(selector, values, preferred_element_type=jnp.float32).astype(jnp.bfloat16)


def shards(
    kv_cache,
    cache_length,
    dest_device,
    dest_slot,
    query_rows,
    new_kv,
    resid_rows,
    norm_gain,
    route_ids,
    route_weight,
    w_gate,
    w_up,
    w_down,
):
    device_count = lax.axis_size("ep")
    owned_count = kv_cache.shape[0]
    group_rows = owned_count // SPAN
    sender = order_matrix(dest_device, device_count, owned_count, group_rows)
    sender_int = sender.astype(jnp.int32)
    sender_bf = sender.astype(jnp.bfloat16)
    ordered = apply_rows(sender_bf, kv_cache.reshape(owned_count, -1)).reshape(SPAN, group_rows, -1)
    slot_meta = (jnp.sum(sender_int * (dest_slot + 1)[None, :], axis=1) - 1).reshape(
        SPAN, group_rows
    )
    length_meta = jnp.sum(sender_int * cache_length[None, :], axis=1).reshape(SPAN, group_rows)
    slot_range = jnp.arange(owned_count, dtype=jnp.int32)[:, None]
    cache_pieces = [ordered[0]]
    slot_pieces = [slot_meta[0]]
    length_pieces = [length_meta[0]]
    for offset in range(1, SPAN):
        got_cache, got_slot, got_length = from_behind(
            (ordered[offset], slot_meta[offset], length_meta[offset]), "ep", offset
        )
        cache_pieces.append(got_cache)
        slot_pieces.append(got_slot)
        length_pieces.append(got_length)
    incoming = jnp.concatenate(cache_pieces, axis=0)
    arrived_slot = jnp.concatenate(slot_pieces, axis=0)
    arrived_length = jnp.concatenate(length_pieces, axis=0)
    chooser = arrived_slot.reshape(1, owned_count) == slot_range
    moved_cache = apply_rows(chooser.astype(jnp.bfloat16), incoming).reshape(kv_cache.shape)
    moved_length = jnp.sum(
        chooser.astype(jnp.int32) * arrived_length.reshape(1, owned_count), axis=1
    )
    context = attend(query_rows, new_kv, moved_cache, moved_length)
    summed_state = resid_rows.astype(jnp.float32) + context.astype(jnp.float32)
    inverse = lax.rsqrt(jnp.mean(summed_state * summed_state, axis=1, keepdims=True) + 1e-06)
    normed = (summed_state * inverse * norm_gain.astype(jnp.float32)[None, :]).astype(jnp.bfloat16)
    experts = device_count // 2
    hits = route_ids[:, :, None] == jnp.arange(experts, dtype=jnp.int32)[None, None, :]
    table = jnp.sum(
        jnp.where(hits, route_weight.astype(jnp.float32)[:, :, None], 0.0), axis=1
    ).astype(jnp.bfloat16)
    all_tables = lax.all_gather(table, "ep", axis=0, tiled=True)
    mine = jnp.arange(experts, dtype=jnp.int32) == lax.axis_index("ep") // 2
    share = jnp.sum(
        jnp.where(mine[None, :], all_tables.astype(jnp.float32), 0.0), axis=1, keepdims=True
    )
    all_rows = lax.all_gather(normed, "ep", axis=0, tiled=True)
    partial_value = expert_half(all_rows, w_gate[0], w_up[0], w_down[0])
    weighted = (partial_value * share).astype(jnp.bfloat16)
    moe_out = lax.psum_scatter(weighted, "ep", scatter_dimension=0, tiled=True)
    return (moved_cache, context, moe_out)


def solution(mesh):
    placed = (
        P(("groups", "ep"), None, None),
        P(("groups", "ep")),
        P(("groups", "ep")),
        P(("groups", "ep")),
        P(("groups", "ep"), None),
        P(("groups", "ep"), None),
        P(("groups", "ep"), None),
        P(),
        P(("groups", "ep"), None),
        P(("groups", "ep"), None),
        P("ep", None, None),
        P("ep", None, None),
        P("ep", None, None),
    )
    return jax.shard_map(
        shards,
        mesh=mesh,
        in_specs=placed,
        out_specs=(
            P(("groups", "ep"), None, None),
            P(("groups", "ep"), None),
            P(("groups", "ep"), None),
        ),
        check_vma=False,
    )
```

```python
import functools
import math

import jax
import jax.numpy as jnp
from jax import lax
from jax.experimental import pallas as pl
from jax.experimental.pallas import tpu as pltpu
from jax.sharding import PartitionSpec as P

HEAD_DIM = 128
Q_HEADS = 32
KV_HEADS = 2
TOPK = 8
SPAN = 4
LEN = 32


def from_behind(array, axis, by):
    peers = lax.axis_size(axis)
    return lax.ppermute(array, axis, [(i, (i + by) % peers) for i in range(peers)])


def attend(query_rows, new_kv, kv_cache, cache_length):
    row_count = query_rows.shape[0]
    group_size = Q_HEADS // KV_HEADS
    score_scale = 1.0 / math.sqrt(HEAD_DIM)
    queries = query_rows.reshape(row_count, KV_HEADS, group_size, HEAD_DIM)
    stored = kv_cache.reshape(row_count, LEN, 2, KV_HEADS, HEAD_DIM)
    fresh = new_kv.reshape(row_count, 2, KV_HEADS, HEAD_DIM)
    scores = (
        jnp.einsum("rgjd,rtgd->rgjt", queries, stored[:, :, 0], preferred_element_type=jnp.float32)
        * score_scale
    )
    own_score = (
        jnp.einsum("rgjd,rgd->rgj", queries, fresh[:, 0], preferred_element_type=jnp.float32)
        * score_scale
    )
    in_range = (jnp.arange(LEN, dtype=jnp.int32)[None, :] < cache_length[:, None])[:, None, None, :]
    masked = jnp.where(in_range, scores, -jnp.inf)
    peak = jnp.maximum(jnp.max(masked, axis=-1), own_score)
    weights = jnp.where(in_range, jnp.exp(scores - peak[..., None]), 0.0)
    own_weight = jnp.exp(own_score - peak)
    denominator = jnp.sum(weights, axis=-1) + own_weight
    probs = (weights / denominator[..., None]).astype(jnp.bfloat16)
    own_prob = (own_weight / denominator).astype(jnp.bfloat16)
    context = jnp.einsum(
        "rgjt,rtgd->rgjd", probs, stored[:, :, 1], preferred_element_type=jnp.float32
    )
    context = (
        context
        + own_prob.astype(jnp.float32)[..., None] * fresh[:, 1].astype(jnp.float32)[:, :, None, :]
    )
    return context.reshape(row_count, Q_HEADS * HEAD_DIM).astype(jnp.bfloat16)


TABLE = 256


def bit_orders(bits):
    down = list(reversed(range(bits)))
    swapped = down[:-2] + [down[-1], down[-2]]
    early = [0, 1] + list(reversed(range(2, bits)))
    return (down, swapped, early)


def relative(order, place):
    return sum(1 << order[j] for j in range(len(order)) if place >> j & 1)


def widths(half):
    tiles = half // 128
    first = (tiles - 2) // 3
    second = (tiles - first) // 2
    gather = (first * 128, second * 128, (tiles - first - second) * 128)
    third = tiles // 3
    rest = (tiles - third) // 2
    scatter = (third * 128, rest * 128, (tiles - third - rest) * 128)
    return gather, scatter


def fold_wide(value):
    cut = value.shape[1] // 2
    return jnp.concatenate([value[:, :cut], value[:, cut:]], axis=0)


def unfold_wide(value):
    cut = value.shape[0] // 2
    return jnp.concatenate([value[:cut], value[cut:]], axis=1)


def expert_kernel(
    bits,
    folded_ref,
    gate_hbm,
    up_hbm,
    down_hbm,
    out_ref,
    gate_ref,
    up_ref,
    down_ref,
    stage,
    last_send,
    last_recv,
    gate_sum,
    up_sum,
    g0,
    g1,
    g2,
    o0,
    o1,
    o2,
    s0,
    s1,
    s2,
    d0,
    d1,
    d2,
    a0,
    a1,
    a2,
    e0,
    e1,
    e2,
    load_sem,
    pair_send,
    pair_recv,
    step_send,
    step_recv,
):
    chips = 1 << bits
    width = down_ref.shape[1]
    half = width // 2
    gather, scatter = widths(half)
    orders = bit_orders(bits)
    held, other = (g0, g1, g2), (o0, o1, o2)
    given, taken, total, landed = (s0, s1, s2), (d0, d1, d2), (a0, a1, a2), (e0, e1, e2)
    me = lax.axis_index("ep")
    chip = me // 2
    core = me % 2
    mate = me + 1 - 2 * core
    far = []
    for bit in range(bits):
        own_bit = (chip // (1 << bit)) % 2
        far.append(me + (1 - 2 * own_bit) * (2 << bit))

    loads = []
    for k, (src, dst) in enumerate(
        ((gate_hbm, gate_ref), (up_hbm, up_ref), (down_hbm, down_ref))
    ):
        load = pltpu.make_async_copy(src.at[0], dst, load_sem.at[k])
        load.start()
        loads.append(load)

    barrier = pltpu.get_barrier_semaphore()
    for target in [mate] + far:
        pl.semaphore_signal(barrier, inc=1, device_id={"ep": target})
    pl.semaphore_wait(barrier, 1 + bits)

    def send(src, dst, send_sem, recv_sem, target):
        copy = pltpu.make_async_remote_copy(
            src_ref=src,
            dst_ref=dst,
            send_sem=send_sem,
            recv_sem=recv_sem,
            device_id={"ep": target},
        )
        copy.start()
        return copy

    sent = []
    first = send(folded_ref.at[1 - core], stage, pair_send.at[0], pair_recv.at[0], mate)
    sent.append(first)
    mine = unfold_wide(folded_ref[core].astype(jnp.float32))
    first.wait_recv()
    theirs = unfold_wide(stage[...].astype(jnp.float32))
    block = jnp.where(
        core == 0,
        jnp.concatenate([mine, theirs], axis=0),
        jnp.concatenate([theirs, mine], axis=0),
    ).astype(jnp.bfloat16)
    starts = (0, gather[0], gather[0] + gather[1])
    held[0][0] = jnp.concatenate(
        [block[:, : gather[0]], block[:, half:]], axis=1
    )
    for c in (1, 2):
        held[c][0] = block[:, starts[c] : starts[c] + gather[c]]

    steps = {}
    for i in range(bits):
        count = 1 << i
        for c in range(3):
            if i > 0:
                steps[c, i - 1].wait_recv()
            steps[c, i] = send(
                held[c].at[pl.ds(0, count)],
                held[c].at[pl.ds(count, count)],
                step_send.at[c * bits + i],
                step_recv.at[c * bits + i],
                far[orders[c][i]],
            )
            sent.append(steps[c, i])
    loads[0].wait()
    loads[1].wait()

    def operand(buffer, c):
        place = {relative(orders[c], p): p for p in range(chips)}
        return jnp.concatenate([buffer[place[r]] for r in range(chips)], axis=0)

    def accumulate(rows, c, side, fresh):
        base = pl.multiple_of(side * half + starts[c], 128)
        left = rows[:, : gather[c]]
        g = jnp.dot(
            left, gate_ref[pl.ds(base, gather[c]), :], preferred_element_type=jnp.float32
        )
        u = jnp.dot(
            left, up_ref[pl.ds(base, gather[c]), :], preferred_element_type=jnp.float32
        )
        if fresh:
            gate_sum[...] = g
            up_sum[...] = u
        else:
            gate_sum[...] += g
            up_sum[...] += u

    swaps = []
    share = None
    for c in range(3):
        steps[c, bits - 1].wait_recv()
        swap = send(held[c], other[c], pair_send.at[1 + c], pair_recv.at[1 + c], mate)
        swaps.append(swap)
        sent.append(swap)
        rows = operand(held[c], c)
        if c == 0:
            tables = rows[:, gather[0] :].astype(jnp.float32)
            lane = lax.broadcasted_iota(jnp.int32, tables.shape, 1)
            share = jnp.sum(jnp.where(lane == chip, tables, 0.0), axis=1, keepdims=True)
        accumulate(rows, c, core, c == 0)
    for c in range(3):
        swaps[c].wait_recv()
        accumulate(operand(other[c], c), c, 1 - core, False)

    gate = gate_sum[...]
    hidden = (gate * jax.nn.sigmoid(gate) * up_sum[...]).astype(jnp.bfloat16)
    loads[2].wait()
    begins = (0, scatter[0], scatter[0] + scatter[1])

    def down(c, side):
        base = pl.multiple_of(side * half + begins[c], 128)
        return (
            jnp.dot(
                hidden, down_ref[:, pl.ds(base, scatter[c])], preferred_element_type=jnp.float32
            )
            * share
        )

    trades = []
    for c in range(3):
        value = down(c, 1 - core).astype(jnp.bfloat16)
        for p in range(chips):
            r = relative(orders[c], p)
            given[c][p] = value[16 * r : 16 * r + 16]
        trade = send(given[c], taken[c], pair_send.at[4 + c], pair_recv.at[4 + c], mate)
        trades.append(trade)
        sent.append(trade)
    base_sem = 3 * bits
    backs = {}

    def back(c, i):
        count = 1 << i
        backs[c, i] = send(
            total[c].at[pl.ds(count, count)],
            landed[c].at[pl.ds(count, count)],
            step_send.at[base_sem + c * bits + i],
            step_recv.at[base_sem + c * bits + i],
            far[orders[c][i]],
        )
        sent.append(backs[c, i])

    for c in range(3):
        value = down(c, core)
        trades[c].wait_recv()
        for p in reversed(range(chips)):
            r = relative(orders[c], p)
            total[c][p] = (
                value[16 * r : 16 * r + 16] + taken[c][p].astype(jnp.float32)
            ).astype(jnp.bfloat16)
        back(c, bits - 1)
    ends = []
    for i in reversed(range(bits)):
        count = 1 << i
        for c in range(3):
            backs[c, i].wait_recv()
            value = total[c][0:count].astype(jnp.float32) + landed[c][
                count : 2 * count
            ].astype(jnp.float32)
            if i > 0:
                total[c][0:count] = value.astype(jnp.bfloat16)
                back(c, i - 1)
            else:
                ends.append(value[0])
    done = jnp.concatenate(ends, axis=1)
    rows = done.shape[0] // 2
    keep = jnp.where(core == 0, done[:rows], done[rows:])
    pass_on = jnp.where(core == 0, done[rows:], done[:rows])
    last_send[...] = fold_wide(pass_on).astype(jnp.bfloat16)
    final = send(last_send, last_recv, pair_send.at[7], pair_recv.at[7], mate)
    sent.append(final)
    final.wait_recv()
    got = unfold_wide(last_recv[...].astype(jnp.float32))
    out_ref[...] = jnp.where(
        core == 0,
        jnp.concatenate([keep, got], axis=1),
        jnp.concatenate([got, keep], axis=1),
    ).astype(out_ref.dtype)
    for copy in sent:
        copy.wait_send()


def expert_layer(normed, table, w_gate, w_up, w_down):
    devices = lax.axis_size("ep")
    bits = (devices // 2).bit_length() - 1
    chips = 1 << bits
    rows, width = normed.shape
    half = width // 2
    gather, scatter = widths(half)
    padded = jnp.pad(table, ((0, 0), (0, TABLE - table.shape[1])))
    folded = jnp.stack(
        [
            fold_wide(jnp.concatenate([normed[:, h * half : (h + 1) * half], padded], axis=1))
            for h in (0, 1)
        ]
    )
    both = 2 * rows
    bf = jnp.bfloat16
    gather_shapes = [
        pltpu.VMEM((chips, both, gather[c] + (TABLE if c == 0 else 0)), bf) for c in range(3)
    ]
    scatter_shapes = [pltpu.VMEM((chips, both, scatter[c]), bf) for c in range(3)]
    hidden_count = w_gate.shape[2]
    return pl.pallas_call(
        functools.partial(expert_kernel, bits),
        out_shape=jax.ShapeDtypeStruct((rows, width), bf),
        in_specs=[pl.BlockSpec(memory_space=pltpu.VMEM)]
        + [pl.BlockSpec(memory_space=pl.ANY)] * 3,
        out_specs=pl.BlockSpec(memory_space=pltpu.VMEM),
        scratch_shapes=[
            pltpu.VMEM(w_gate.shape[1:], bf),
            pltpu.VMEM(w_up.shape[1:], bf),
            pltpu.VMEM(w_down.shape[1:], bf),
            pltpu.VMEM((both, (half + TABLE) // 2), bf),
            pltpu.VMEM((both, half // 2), bf),
            pltpu.VMEM((both, half // 2), bf),
            pltpu.VMEM((chips * both, hidden_count), jnp.float32),
            pltpu.VMEM((chips * both, hidden_count), jnp.float32),
        ]
        + gather_shapes * 2
        + scatter_shapes * 4
        + [
            pltpu.SemaphoreType.DMA((3,)),
            pltpu.SemaphoreType.DMA((8,)),
            pltpu.SemaphoreType.DMA((8,)),
            pltpu.SemaphoreType.DMA((6 * bits,)),
            pltpu.SemaphoreType.DMA((6 * bits,)),
        ],
        compiler_params=pltpu.CompilerParams(
            collective_id=0, has_side_effects=True, vmem_limit_bytes=56 * 1024 * 1024
        ),
    )(folded, w_gate, w_up, w_down)


def order_matrix(dest_device, device_count, owned_count, group_rows):
    offset = (dest_device - lax.axis_index("ep")) % device_count
    onehot = (offset[:, None] == jnp.arange(SPAN, dtype=jnp.int32)[None, :]).astype(jnp.int32)
    rank = jnp.sum((jnp.cumsum(onehot, axis=0) - onehot) * onehot, axis=1)
    position = offset * group_rows + rank
    return jnp.arange(owned_count, dtype=jnp.int32)[:, None] == position[None, :]


def apply_rows(selector, values):
    return jnp.dot(selector, values, preferred_element_type=jnp.float32).astype(jnp.bfloat16)


def shards(
    kv_cache,
    cache_length,
    dest_device,
    dest_slot,
    query_rows,
    new_kv,
    resid_rows,
    norm_gain,
    route_ids,
    route_weight,
    w_gate,
    w_up,
    w_down,
):
    device_count = lax.axis_size("ep")
    owned_count = kv_cache.shape[0]
    group_rows = owned_count // SPAN
    sender = order_matrix(dest_device, device_count, owned_count, group_rows)
    sender_int = sender.astype(jnp.int32)
    sender_bf = sender.astype(jnp.bfloat16)
    ordered = apply_rows(sender_bf, kv_cache.reshape(owned_count, -1)).reshape(SPAN, group_rows, -1)
    slot_meta = (jnp.sum(sender_int * (dest_slot + 1)[None, :], axis=1) - 1).reshape(
        SPAN, group_rows
    )
    length_meta = jnp.sum(sender_int * cache_length[None, :], axis=1).reshape(SPAN, group_rows)
    slot_range = jnp.arange(owned_count, dtype=jnp.int32)[:, None]
    cache_pieces = [ordered[0]]
    slot_pieces = [slot_meta[0]]
    length_pieces = [length_meta[0]]
    for offset in range(1, SPAN):
        got_cache, got_slot, got_length = from_behind(
            (ordered[offset], slot_meta[offset], length_meta[offset]), "ep", offset
        )
        cache_pieces.append(got_cache)
        slot_pieces.append(got_slot)
        length_pieces.append(got_length)
    incoming = jnp.concatenate(cache_pieces, axis=0)
    arrived_slot = jnp.concatenate(slot_pieces, axis=0)
    arrived_length = jnp.concatenate(length_pieces, axis=0)
    chooser = arrived_slot.reshape(1, owned_count) == slot_range
    moved_cache = apply_rows(chooser.astype(jnp.bfloat16), incoming).reshape(kv_cache.shape)
    moved_length = jnp.sum(
        chooser.astype(jnp.int32) * arrived_length.reshape(1, owned_count), axis=1
    )
    context = attend(query_rows, new_kv, moved_cache, moved_length)
    summed_state = resid_rows.astype(jnp.float32) + context.astype(jnp.float32)
    inverse = lax.rsqrt(jnp.mean(summed_state * summed_state, axis=1, keepdims=True) + 1e-06)
    normed = (summed_state * inverse * norm_gain.astype(jnp.float32)[None, :]).astype(jnp.bfloat16)
    experts = device_count // 2
    hits = route_ids[:, :, None] == jnp.arange(experts, dtype=jnp.int32)[None, None, :]
    table = jnp.sum(
        jnp.where(hits, route_weight.astype(jnp.float32)[:, :, None], 0.0), axis=1
    ).astype(jnp.bfloat16)
    moe_out = expert_layer(normed, table, w_gate, w_up, w_down)
    return (moved_cache, context, moe_out)


def solution(mesh):
    placed = (
        P(("groups", "ep"), None, None),
        P(("groups", "ep")),
        P(("groups", "ep")),
        P(("groups", "ep")),
        P(("groups", "ep"), None),
        P(("groups", "ep"), None),
        P(("groups", "ep"), None),
        P(),
        P(("groups", "ep"), None),
        P(("groups", "ep"), None),
        P("ep", None, None),
        P("ep", None, None),
        P("ep", None, None),
    )
    return jax.shard_map(
        shards,
        mesh=mesh,
        in_specs=placed,
        out_specs=(
            P(("groups", "ep"), None, None),
            P(("groups", "ep"), None),
            P(("groups", "ep"), None),
        ),
        check_vma=False,
    )
```

```python
import functools
import math

import jax
import jax.numpy as jnp
from jax import lax
from jax.experimental import pallas as pl
from jax.experimental.pallas import tpu as pltpu
from jax.sharding import PartitionSpec as P

HEAD_DIM = 128
Q_HEADS = 32
KV_HEADS = 2
TOPK = 8
SPAN = 4
LEN = 32


def attend(query_rows, new_kv, kv_cache, cache_length):
    row_count = query_rows.shape[0]
    group_size = Q_HEADS // KV_HEADS
    score_scale = 1.0 / math.sqrt(HEAD_DIM)
    queries = query_rows.reshape(row_count, KV_HEADS, group_size, HEAD_DIM)
    stored = kv_cache.reshape(row_count, LEN, 2, KV_HEADS, HEAD_DIM)
    fresh = new_kv.reshape(row_count, 2, KV_HEADS, HEAD_DIM)
    scores = (
        jnp.einsum("rgjd,rtgd->rgjt", queries, stored[:, :, 0], preferred_element_type=jnp.float32)
        * score_scale
    )
    own_score = (
        jnp.einsum("rgjd,rgd->rgj", queries, fresh[:, 0], preferred_element_type=jnp.float32)
        * score_scale
    )
    in_range = (jnp.arange(LEN, dtype=jnp.int32)[None, :] < cache_length[:, None])[:, None, None, :]
    masked = jnp.where(in_range, scores, -jnp.inf)
    peak = jnp.maximum(jnp.max(masked, axis=-1), own_score)
    weights = jnp.where(in_range, jnp.exp(scores - peak[..., None]), 0.0)
    own_weight = jnp.exp(own_score - peak)
    denominator = jnp.sum(weights, axis=-1) + own_weight
    probs = (weights / denominator[..., None]).astype(jnp.bfloat16)
    own_prob = (own_weight / denominator).astype(jnp.bfloat16)
    context = jnp.einsum(
        "rgjt,rtgd->rgjd", probs, stored[:, :, 1], preferred_element_type=jnp.float32
    )
    context = (
        context
        + own_prob.astype(jnp.float32)[..., None] * fresh[:, 1].astype(jnp.float32)[:, :, None, :]
    )
    return context.reshape(row_count, Q_HEADS * HEAD_DIM).astype(jnp.bfloat16)


TABLE = 256


def bit_orders(bits):
    down = list(reversed(range(bits)))
    swapped = down[:-2] + [down[-1], down[-2]]
    early = [0, 1] + list(reversed(range(2, bits)))
    return (down, swapped, early)


def relative(order, place):
    return sum(1 << order[j] for j in range(len(order)) if place >> j & 1)


def widths(half):
    tiles = half // 128
    first = (tiles - 2) // 3
    second = (tiles - first) // 2
    gather = (first * 128, second * 128, (tiles - first - second) * 128)
    third = tiles // 3
    rest = (tiles - third) // 2
    scatter = (third * 128, rest * 128, (tiles - third - rest) * 128)
    return gather, scatter


def fold_wide(value):
    cut = value.shape[1] // 2
    return jnp.concatenate([value[:, :cut], value[:, cut:]], axis=0)


def unfold_wide(value):
    cut = value.shape[0] // 2
    return jnp.concatenate([value[:cut], value[cut:]], axis=1)


def expert_kernel(
    bits,
    folded_ref,
    gate_hbm,
    up_hbm,
    down_hbm,
    out_ref,
    gate_ref,
    up_ref,
    down_ref,
    stage,
    last_send,
    last_recv,
    gate_sum,
    up_sum,
    g0,
    g1,
    g2,
    o0,
    o1,
    o2,
    s0,
    s1,
    s2,
    d0,
    d1,
    d2,
    a0,
    a1,
    a2,
    e0,
    e1,
    e2,
    load_sem,
    pair_send,
    pair_recv,
    step_send,
    step_recv,
):
    chips = 1 << bits
    width = down_ref.shape[1]
    half = width // 2
    gather, scatter = widths(half)
    orders = bit_orders(bits)
    held, other = (g0, g1, g2), (o0, o1, o2)
    given, taken, total, landed = (s0, s1, s2), (d0, d1, d2), (a0, a1, a2), (e0, e1, e2)
    me = lax.axis_index("ep")
    chip = me // 2
    core = me % 2
    mate = me + 1 - 2 * core
    far = []
    for bit in range(bits):
        own_bit = (chip // (1 << bit)) % 2
        far.append(me + (1 - 2 * own_bit) * (2 << bit))

    loads = []
    for k, (src, dst) in enumerate(
        ((gate_hbm, gate_ref), (up_hbm, up_ref), (down_hbm, down_ref))
    ):
        load = pltpu.make_async_copy(src.at[0], dst, load_sem.at[k])
        load.start()
        loads.append(load)

    barrier = pltpu.get_barrier_semaphore()
    for target in [mate] + far:
        pl.semaphore_signal(barrier, inc=1, device_id={"ep": target})
    pl.semaphore_wait(barrier, 1 + bits)

    def send(src, dst, send_sem, recv_sem, target):
        copy = pltpu.make_async_remote_copy(
            src_ref=src,
            dst_ref=dst,
            send_sem=send_sem,
            recv_sem=recv_sem,
            device_id={"ep": target},
        )
        copy.start()
        return copy

    sent = []
    first = send(folded_ref.at[1 - core], stage, pair_send.at[0], pair_recv.at[0], mate)
    sent.append(first)
    mine = unfold_wide(folded_ref[core].astype(jnp.float32))
    first.wait_recv()
    theirs = unfold_wide(stage[...].astype(jnp.float32))
    block = jnp.where(
        core == 0,
        jnp.concatenate([mine, theirs], axis=0),
        jnp.concatenate([theirs, mine], axis=0),
    ).astype(jnp.bfloat16)
    starts = (0, gather[0], gather[0] + gather[1])
    held[0][0] = jnp.concatenate(
        [block[:, : gather[0]], block[:, half:]], axis=1
    )
    for c in (1, 2):
        held[c][0] = block[:, starts[c] : starts[c] + gather[c]]

    steps = {}
    for i in range(bits):
        count = 1 << i
        for c in range(3):
            if i > 0:
                steps[c, i - 1].wait_recv()
            steps[c, i] = send(
                held[c].at[pl.ds(0, count)],
                held[c].at[pl.ds(count, count)],
                step_send.at[c * bits + i],
                step_recv.at[c * bits + i],
                far[orders[c][i]],
            )
            sent.append(steps[c, i])
    loads[0].wait()
    loads[1].wait()

    def operand(buffer, c):
        place = {relative(orders[c], p): p for p in range(chips)}
        return jnp.concatenate([buffer[place[r]] for r in range(chips)], axis=0)

    def accumulate(rows, c, side, fresh):
        base = pl.multiple_of(side * half + starts[c], 128)
        left = rows[:, : gather[c]]
        g = jnp.dot(
            left, gate_ref[pl.ds(base, gather[c]), :], preferred_element_type=jnp.float32
        )
        u = jnp.dot(
            left, up_ref[pl.ds(base, gather[c]), :], preferred_element_type=jnp.float32
        )
        if fresh:
            gate_sum[...] = g
            up_sum[...] = u
        else:
            gate_sum[...] += g
            up_sum[...] += u

    swaps = []
    share = None
    for c in range(3):
        steps[c, bits - 1].wait_recv()
        swap = send(held[c], other[c], pair_send.at[1 + c], pair_recv.at[1 + c], mate)
        swaps.append(swap)
        sent.append(swap)
        rows = operand(held[c], c)
        if c == 0:
            tables = rows[:, gather[0] :].astype(jnp.float32)
            lane = lax.broadcasted_iota(jnp.int32, tables.shape, 1)
            share = jnp.sum(jnp.where(lane == chip, tables, 0.0), axis=1, keepdims=True)
        accumulate(rows, c, core, c == 0)
    for c in range(3):
        swaps[c].wait_recv()
        accumulate(operand(other[c], c), c, 1 - core, False)

    gate = gate_sum[...]
    hidden = (gate * jax.nn.sigmoid(gate) * up_sum[...]).astype(jnp.bfloat16)
    loads[2].wait()
    begins = (0, scatter[0], scatter[0] + scatter[1])

    def down(c, side):
        base = pl.multiple_of(side * half + begins[c], 128)
        return (
            jnp.dot(
                hidden, down_ref[:, pl.ds(base, scatter[c])], preferred_element_type=jnp.float32
            )
            * share
        )

    trades = []
    for c in range(3):
        value = down(c, 1 - core).astype(jnp.bfloat16)
        for p in range(chips):
            r = relative(orders[c], p)
            given[c][p] = value[16 * r : 16 * r + 16]
        trade = send(given[c], taken[c], pair_send.at[4 + c], pair_recv.at[4 + c], mate)
        trades.append(trade)
        sent.append(trade)
    base_sem = 3 * bits
    backs = {}

    def back(c, i):
        count = 1 << i
        backs[c, i] = send(
            total[c].at[pl.ds(count, count)],
            landed[c].at[pl.ds(count, count)],
            step_send.at[base_sem + c * bits + i],
            step_recv.at[base_sem + c * bits + i],
            far[orders[c][i]],
        )
        sent.append(backs[c, i])

    for c in range(3):
        value = down(c, core)
        trades[c].wait_recv()
        for p in reversed(range(chips)):
            r = relative(orders[c], p)
            total[c][p] = (
                value[16 * r : 16 * r + 16] + taken[c][p].astype(jnp.float32)
            ).astype(jnp.bfloat16)
        back(c, bits - 1)
    ends = []
    for i in reversed(range(bits)):
        count = 1 << i
        for c in range(3):
            backs[c, i].wait_recv()
            value = total[c][0:count].astype(jnp.float32) + landed[c][
                count : 2 * count
            ].astype(jnp.float32)
            if i > 0:
                total[c][0:count] = value.astype(jnp.bfloat16)
                back(c, i - 1)
            else:
                ends.append(value[0])
    done = jnp.concatenate(ends, axis=1)
    rows = done.shape[0] // 2
    keep = jnp.where(core == 0, done[:rows], done[rows:])
    pass_on = jnp.where(core == 0, done[rows:], done[:rows])
    last_send[...] = fold_wide(pass_on).astype(jnp.bfloat16)
    final = send(last_send, last_recv, pair_send.at[7], pair_recv.at[7], mate)
    sent.append(final)
    final.wait_recv()
    got = unfold_wide(last_recv[...].astype(jnp.float32))
    out_ref[...] = jnp.where(
        core == 0,
        jnp.concatenate([keep, got], axis=1),
        jnp.concatenate([got, keep], axis=1),
    ).astype(out_ref.dtype)
    for copy in sent:
        copy.wait_send()


def expert_layer(normed, table, w_gate, w_up, w_down):
    devices = lax.axis_size("ep")
    bits = (devices // 2).bit_length() - 1
    chips = 1 << bits
    rows, width = normed.shape
    half = width // 2
    gather, scatter = widths(half)
    padded = jnp.pad(table, ((0, 0), (0, TABLE - table.shape[1])))
    folded = jnp.stack(
        [
            fold_wide(jnp.concatenate([normed[:, h * half : (h + 1) * half], padded], axis=1))
            for h in (0, 1)
        ]
    )
    both = 2 * rows
    bf = jnp.bfloat16
    gather_shapes = [
        pltpu.VMEM((chips, both, gather[c] + (TABLE if c == 0 else 0)), bf) for c in range(3)
    ]
    scatter_shapes = [pltpu.VMEM((chips, both, scatter[c]), bf) for c in range(3)]
    hidden_count = w_gate.shape[2]
    return pl.pallas_call(
        functools.partial(expert_kernel, bits),
        out_shape=jax.ShapeDtypeStruct((rows, width), bf),
        in_specs=[pl.BlockSpec(memory_space=pltpu.VMEM)]
        + [pl.BlockSpec(memory_space=pl.ANY)] * 3,
        out_specs=pl.BlockSpec(memory_space=pltpu.VMEM),
        scratch_shapes=[
            pltpu.VMEM(w_gate.shape[1:], bf),
            pltpu.VMEM(w_up.shape[1:], bf),
            pltpu.VMEM(w_down.shape[1:], bf),
            pltpu.VMEM((both, (half + TABLE) // 2), bf),
            pltpu.VMEM((both, half // 2), bf),
            pltpu.VMEM((both, half // 2), bf),
            pltpu.VMEM((chips * both, hidden_count), jnp.float32),
            pltpu.VMEM((chips * both, hidden_count), jnp.float32),
        ]
        + gather_shapes * 2
        + scatter_shapes * 4
        + [
            pltpu.SemaphoreType.DMA((3,)),
            pltpu.SemaphoreType.DMA((8,)),
            pltpu.SemaphoreType.DMA((8,)),
            pltpu.SemaphoreType.DMA((6 * bits,)),
            pltpu.SemaphoreType.DMA((6 * bits,)),
        ],
        compiler_params=pltpu.CompilerParams(
            collective_id=0, has_side_effects=True, vmem_limit_bytes=56 * 1024 * 1024
        ),
    )(folded, w_gate, w_up, w_down)


def migrate_kernel(
    peers,
    dest_ref,
    slot_ref,
    length_ref,
    cache_ref,
    arrived_ref,
    meta_ref,
    cache_out,
    cache_in,
    meta_out,
    meta_in,
    cache_send,
    cache_recv,
    meta_send,
    meta_recv,
):
    me = lax.axis_index("ep")
    owned = cache_ref.shape[0]
    per = owned // SPAN
    ahead = [lax.rem(me + o, peers) for o in range(SPAN)]
    behind = [lax.rem(me + peers - o, peers) for o in range(SPAN)]
    barrier = pltpu.get_barrier_semaphore()
    for o in range(1, SPAN):
        pl.semaphore_signal(barrier, inc=1, device_id={"ep": ahead[o]})
        pl.semaphore_signal(barrier, inc=1, device_id={"ep": behind[o]})

    counts = [jnp.int32(0)] * SPAN
    chosen = [[jnp.int32(0)] * per for _ in range(SPAN)]
    for i in range(owned):
        gap = dest_ref[i] - me
        gap = jnp.where(gap < 0, gap + peers, gap)
        for o in range(SPAN):
            here = gap == o
            for k in range(per):
                chosen[o][k] = jnp.where(here & (counts[o] == k), i, chosen[o][k])
            counts[o] = counts[o] + here.astype(jnp.int32)
    lane = lax.broadcasted_iota(jnp.int32, meta_out.shape[1:], 1)

    def describe(o):
        tile = jnp.zeros(meta_out.shape[1:], jnp.int32)
        for k in range(per):
            tile = jnp.where(lane == k, slot_ref[chosen[o][k]], tile)
            tile = jnp.where(lane == per + k, length_ref[chosen[o][k]], tile)
        return tile

    for o in range(1, SPAN):
        for k in range(per):
            cache_out[o - 1, k] = cache_ref[chosen[o][k]]
        meta_out[o - 1] = describe(o)
    pl.semaphore_wait(barrier, 2 * (SPAN - 1))
    copies = []
    for o in range(SPAN - 1, 0, -1):
        for src, dst, send_sem, recv_sem in (
            (cache_out, cache_in, cache_send, cache_recv),
            (meta_out, meta_in, meta_send, meta_recv),
        ):
            copy = pltpu.make_async_remote_copy(
                src_ref=src.at[o - 1],
                dst_ref=dst.at[o - 1],
                send_sem=send_sem.at[o - 1],
                recv_sem=recv_sem.at[o - 1],
                device_id={"ep": ahead[o]},
            )
            copy.start()
            copies.append(copy)
    for k in range(per):
        arrived_ref[k] = cache_ref[chosen[0][k]]
    meta_ref[0] = describe(0)
    for copy in copies:
        copy.wait_recv()
    for o in range(1, SPAN):
        for k in range(per):
            arrived_ref[o * per + k] = cache_in[o - 1, k]
        meta_ref[o] = meta_in[o - 1]
    for copy in copies:
        copy.wait_send()


def migrate(kv_cache, cache_length, dest_device, dest_slot):
    peers = lax.axis_size("ep")
    per = kv_cache.shape[0] // SPAN
    piece = pltpu.VMEM((SPAN - 1, per) + kv_cache.shape[1:], kv_cache.dtype)
    note = pltpu.VMEM((SPAN - 1, 8, 128), jnp.int32)
    smem = pl.BlockSpec(memory_space=pltpu.SMEM)
    vmem = pl.BlockSpec(memory_space=pltpu.VMEM)
    arrived, meta = pl.pallas_call(
        functools.partial(migrate_kernel, peers),
        out_shape=(
            jax.ShapeDtypeStruct(kv_cache.shape, kv_cache.dtype),
            jax.ShapeDtypeStruct((SPAN, 8, 128), jnp.int32),
        ),
        in_specs=[smem, smem, smem, vmem],
        out_specs=(vmem, vmem),
        scratch_shapes=[piece, piece, note, note]
        + [pltpu.SemaphoreType.DMA((SPAN - 1,))] * 4,
        compiler_params=pltpu.CompilerParams(
            collective_id=1, has_side_effects=True, vmem_limit_bytes=16 * 1024 * 1024
        ),
    )(dest_device, dest_slot, cache_length, kv_cache)
    return arrived, meta[:, 0, :per], meta[:, 0, per : 2 * per]


def apply_rows(selector, values):
    return jnp.dot(selector, values, preferred_element_type=jnp.float32).astype(jnp.bfloat16)


def shards(
    kv_cache,
    cache_length,
    dest_device,
    dest_slot,
    query_rows,
    new_kv,
    resid_rows,
    norm_gain,
    route_ids,
    route_weight,
    w_gate,
    w_up,
    w_down,
):
    device_count = lax.axis_size("ep")
    owned_count = kv_cache.shape[0]
    incoming, arrived_slot, arrived_length = migrate(
        kv_cache, cache_length, dest_device, dest_slot
    )
    incoming = incoming.reshape(owned_count, -1)
    slot_range = jnp.arange(owned_count, dtype=jnp.int32)[:, None]
    chooser = arrived_slot.reshape(1, owned_count) == slot_range
    moved_cache = apply_rows(chooser.astype(jnp.bfloat16), incoming).reshape(kv_cache.shape)
    moved_length = jnp.sum(
        chooser.astype(jnp.int32) * arrived_length.reshape(1, owned_count), axis=1
    )
    context = attend(query_rows, new_kv, moved_cache, moved_length)
    summed_state = resid_rows.astype(jnp.float32) + context.astype(jnp.float32)
    inverse = lax.rsqrt(jnp.mean(summed_state * summed_state, axis=1, keepdims=True) + 1e-06)
    normed = (summed_state * inverse * norm_gain.astype(jnp.float32)[None, :]).astype(jnp.bfloat16)
    experts = device_count // 2
    hits = route_ids[:, :, None] == jnp.arange(experts, dtype=jnp.int32)[None, None, :]
    table = jnp.sum(
        jnp.where(hits, route_weight.astype(jnp.float32)[:, :, None], 0.0), axis=1
    ).astype(jnp.bfloat16)
    moe_out = expert_layer(normed, table, w_gate, w_up, w_down)
    return (moved_cache, context, moe_out)


def solution(mesh):
    placed = (
        P(("groups", "ep"), None, None),
        P(("groups", "ep")),
        P(("groups", "ep")),
        P(("groups", "ep")),
        P(("groups", "ep"), None),
        P(("groups", "ep"), None),
        P(("groups", "ep"), None),
        P(),
        P(("groups", "ep"), None),
        P(("groups", "ep"), None),
        P("ep", None, None),
        P("ep", None, None),
        P("ep", None, None),
    )
    return jax.shard_map(
        shards,
        mesh=mesh,
        in_specs=placed,
        out_specs=(
            P(("groups", "ep"), None, None),
            P(("groups", "ep"), None),
            P(("groups", "ep"), None),
        ),
        check_vma=False,
    )
```

```python
import functools
import math

import jax
import jax.numpy as jnp
from jax import lax
from jax.experimental import pallas as pl
from jax.experimental.pallas import tpu as pltpu
from jax.sharding import PartitionSpec as P

HEAD_DIM = 128
Q_HEADS = 32
KV_HEADS = 2
TOPK = 8
SPAN = 4
LEN = 32


def attend(query_rows, new_kv, kv_cache, cache_length):
    row_count = query_rows.shape[0]
    group_size = Q_HEADS // KV_HEADS
    score_scale = 1.0 / math.sqrt(HEAD_DIM)
    queries = query_rows.reshape(row_count, KV_HEADS, group_size, HEAD_DIM)
    stored = kv_cache.reshape(row_count, LEN, 2, KV_HEADS, HEAD_DIM)
    fresh = new_kv.reshape(row_count, 2, KV_HEADS, HEAD_DIM)
    scores = (
        jnp.einsum("rgjd,rtgd->rgjt", queries, stored[:, :, 0], preferred_element_type=jnp.float32)
        * score_scale
    )
    own_score = (
        jnp.einsum("rgjd,rgd->rgj", queries, fresh[:, 0], preferred_element_type=jnp.float32)
        * score_scale
    )
    in_range = (jnp.arange(LEN, dtype=jnp.int32)[None, :] < cache_length[:, None])[:, None, None, :]
    masked = jnp.where(in_range, scores, -jnp.inf)
    peak = jnp.maximum(jnp.max(masked, axis=-1), own_score)
    weights = jnp.where(in_range, jnp.exp(scores - peak[..., None]), 0.0)
    own_weight = jnp.exp(own_score - peak)
    denominator = jnp.sum(weights, axis=-1) + own_weight
    probs = (weights / denominator[..., None]).astype(jnp.bfloat16)
    own_prob = (own_weight / denominator).astype(jnp.bfloat16)
    context = jnp.einsum(
        "rgjt,rtgd->rgjd", probs, stored[:, :, 1], preferred_element_type=jnp.float32
    )
    context = (
        context
        + own_prob.astype(jnp.float32)[..., None] * fresh[:, 1].astype(jnp.float32)[:, :, None, :]
    )
    return context.reshape(row_count, Q_HEADS * HEAD_DIM).astype(jnp.bfloat16)


TABLE = 256


def bit_orders(bits):
    down = list(reversed(range(bits)))
    swapped = down[:-2] + [down[-1], down[-2]]
    early = [0, 1] + list(reversed(range(2, bits)))
    return (down, swapped, early)


def relative(order, place):
    return sum(1 << order[j] for j in range(len(order)) if place >> j & 1)


def widths(half):
    tiles = half // 128
    first = (tiles - 2) // 3
    second = (tiles - first) // 2
    gather = (first * 128, second * 128, (tiles - first - second) * 128)
    third = tiles // 3
    rest = (tiles - third) // 2
    scatter = (third * 128, rest * 128, (tiles - third - rest) * 128)
    return gather, scatter


def fold_wide(value):
    cut = value.shape[1] // 2
    return jnp.concatenate([value[:, :cut], value[:, cut:]], axis=0)


def unfold_wide(value):
    cut = value.shape[0] // 2
    return jnp.concatenate([value[:cut], value[cut:]], axis=1)


def expert_kernel(
    bits,
    folded_ref,
    gate_hbm,
    up_hbm,
    down_hbm,
    out_ref,
    gate_ref,
    up_ref,
    down_ref,
    stage,
    last_send,
    last_recv,
    gate_sum,
    up_sum,
    g0,
    g1,
    g2,
    o0,
    o1,
    o2,
    s0,
    s1,
    s2,
    d0,
    d1,
    d2,
    a0,
    a1,
    a2,
    e0,
    e1,
    e2,
    load_sem,
    pair_send,
    pair_recv,
    step_send,
    step_recv,
):
    chips = 1 << bits
    width = down_ref.shape[1]
    half = width // 2
    gather, scatter = widths(half)
    orders = bit_orders(bits)
    held, other = (g0, g1, g2), (o0, o1, o2)
    given, taken, total, landed = (s0, s1, s2), (d0, d1, d2), (a0, a1, a2), (e0, e1, e2)
    me = lax.axis_index("ep")
    chip = me // 2
    core = me % 2
    mate = me + 1 - 2 * core
    far = []
    for bit in range(bits):
        own_bit = (chip // (1 << bit)) % 2
        far.append(me + (1 - 2 * own_bit) * (2 << bit))

    loads = []
    for k, (src, dst) in enumerate(
        ((gate_hbm, gate_ref), (up_hbm, up_ref), (down_hbm, down_ref))
    ):
        load = pltpu.make_async_copy(src.at[0], dst, load_sem.at[k])
        load.start()
        loads.append(load)

    barrier = pltpu.get_barrier_semaphore()
    for target in [mate] + far:
        pl.semaphore_signal(barrier, inc=1, device_id={"ep": target})
    pl.semaphore_wait(barrier, 1 + bits)

    def send(src, dst, send_sem, recv_sem, target):
        copy = pltpu.make_async_remote_copy(
            src_ref=src,
            dst_ref=dst,
            send_sem=send_sem,
            recv_sem=recv_sem,
            device_id={"ep": target},
        )
        copy.start()
        return copy

    sent = []
    first = send(folded_ref.at[1 - core], stage, pair_send.at[0], pair_recv.at[0], mate)
    sent.append(first)
    mine = unfold_wide(folded_ref[core].astype(jnp.float32))
    first.wait_recv()
    theirs = unfold_wide(stage[...].astype(jnp.float32))
    block = jnp.where(
        core == 0,
        jnp.concatenate([mine, theirs], axis=0),
        jnp.concatenate([theirs, mine], axis=0),
    ).astype(jnp.bfloat16)
    starts = (0, gather[0], gather[0] + gather[1])
    held[0][0] = jnp.concatenate(
        [block[:, : gather[0]], block[:, half:]], axis=1
    )
    for c in (1, 2):
        held[c][0] = block[:, starts[c] : starts[c] + gather[c]]

    by_depth = sorted(range(chips), key=lambda p: (p.bit_count(), p))
    hops = {}
    for p in by_depth:
        for c in range(3):
            if p > 0:
                hops[c, p].wait_recv()
            for i in range(p.bit_length(), bits):
                to = p + (1 << i)
                hops[c, to] = send(
                    held[c].at[p],
                    held[c].at[to],
                    step_send.at[c * chips + to],
                    step_recv.at[c * chips + to],
                    far[orders[c][i]],
                )
                sent.append(hops[c, to])
    loads[0].wait()
    loads[1].wait()

    def operand(buffer, c):
        place = {relative(orders[c], p): p for p in range(chips)}
        return jnp.concatenate([buffer[place[r]] for r in range(chips)], axis=0)

    def accumulate(rows, c, side, fresh):
        base = pl.multiple_of(side * half + starts[c], 128)
        left = rows[:, : gather[c]]
        g = jnp.dot(
            left, gate_ref[pl.ds(base, gather[c]), :], preferred_element_type=jnp.float32
        )
        u = jnp.dot(
            left, up_ref[pl.ds(base, gather[c]), :], preferred_element_type=jnp.float32
        )
        if fresh:
            gate_sum[...] = g
            up_sum[...] = u
        else:
            gate_sum[...] += g
            up_sum[...] += u

    swaps = []
    share = None
    for c in range(3):
        swap = send(held[c], other[c], pair_send.at[1 + c], pair_recv.at[1 + c], mate)
        swaps.append(swap)
        sent.append(swap)
        rows = operand(held[c], c)
        if c == 0:
            tables = rows[:, gather[0] :].astype(jnp.float32)
            lane = lax.broadcasted_iota(jnp.int32, tables.shape, 1)
            share = jnp.sum(jnp.where(lane == chip, tables, 0.0), axis=1, keepdims=True)
        accumulate(rows, c, core, c == 0)
    for c in range(3):
        swaps[c].wait_recv()
        accumulate(operand(other[c], c), c, 1 - core, False)

    gate = gate_sum[...]
    hidden = (gate * jax.nn.sigmoid(gate) * up_sum[...]).astype(jnp.bfloat16)
    loads[2].wait()
    begins = (0, scatter[0], scatter[0] + scatter[1])

    def down(c, side):
        base = pl.multiple_of(side * half + begins[c], 128)
        return (
            jnp.dot(
                hidden, down_ref[:, pl.ds(base, scatter[c])], preferred_element_type=jnp.float32
            )
            * share
        )

    trades = []
    for c in range(3):
        value = down(c, 1 - core).astype(jnp.bfloat16)
        for p in range(chips):
            r = relative(orders[c], p)
            given[c][p] = value[16 * r : 16 * r + 16]
        trade = send(given[c], taken[c], pair_send.at[4 + c], pair_recv.at[4 + c], mate)
        trades.append(trade)
        sent.append(trade)
    base_sem = 3 * chips
    backs = {}

    def back(c, p):
        i = p.bit_length() - 1
        backs[c, p] = send(
            total[c].at[p],
            landed[c].at[p],
            step_send.at[base_sem + c * chips + p],
            step_recv.at[base_sem + c * chips + p],
            far[orders[c][i]],
        )
        sent.append(backs[c, p])

    def block_of(p, values, c):
        r = relative(orders[c], p)
        return values[16 * r : 16 * r + 16] + taken[c][p].astype(jnp.float32)

    for c in range(3):
        value = down(c, core)
        trades[c].wait_recv()
        for p in reversed(by_depth):
            total[c][p] = block_of(p, value, c).astype(jnp.bfloat16)
            if p >= chips // 2:
                back(c, p)
    ends = []
    for p in reversed(by_depth):
        if p >= chips // 2:
            continue
        for c in range(3):
            value = total[c][p].astype(jnp.float32)
            for i in reversed(range(p.bit_length(), bits)):
                backs[c, p + (1 << i)].wait_recv()
                value = value + landed[c][p + (1 << i)].astype(jnp.float32)
            if p > 0:
                total[c][p] = value.astype(jnp.bfloat16)
                back(c, p)
            else:
                ends.append(value)
    done = jnp.concatenate(ends, axis=1)
    rows = done.shape[0] // 2
    keep = jnp.where(core == 0, done[:rows], done[rows:])
    pass_on = jnp.where(core == 0, done[rows:], done[:rows])
    last_send[...] = fold_wide(pass_on).astype(jnp.bfloat16)
    final = send(last_send, last_recv, pair_send.at[7], pair_recv.at[7], mate)
    sent.append(final)
    final.wait_recv()
    got = unfold_wide(last_recv[...].astype(jnp.float32))
    out_ref[...] = jnp.where(
        core == 0,
        jnp.concatenate([keep, got], axis=1),
        jnp.concatenate([got, keep], axis=1),
    ).astype(out_ref.dtype)
    for copy in sent:
        copy.wait_send()


def expert_layer(normed, table, w_gate, w_up, w_down):
    devices = lax.axis_size("ep")
    bits = (devices // 2).bit_length() - 1
    chips = 1 << bits
    rows, width = normed.shape
    half = width // 2
    gather, scatter = widths(half)
    padded = jnp.pad(table, ((0, 0), (0, TABLE - table.shape[1])))
    folded = jnp.stack(
        [
            fold_wide(jnp.concatenate([normed[:, h * half : (h + 1) * half], padded], axis=1))
            for h in (0, 1)
        ]
    )
    both = 2 * rows
    bf = jnp.bfloat16
    gather_shapes = [
        pltpu.VMEM((chips, both, gather[c] + (TABLE if c == 0 else 0)), bf) for c in range(3)
    ]
    scatter_shapes = [pltpu.VMEM((chips, both, scatter[c]), bf) for c in range(3)]
    hidden_count = w_gate.shape[2]
    return pl.pallas_call(
        functools.partial(expert_kernel, bits),
        out_shape=jax.ShapeDtypeStruct((rows, width), bf),
        in_specs=[pl.BlockSpec(memory_space=pltpu.VMEM)]
        + [pl.BlockSpec(memory_space=pl.ANY)] * 3,
        out_specs=pl.BlockSpec(memory_space=pltpu.VMEM),
        scratch_shapes=[
            pltpu.VMEM(w_gate.shape[1:], bf),
            pltpu.VMEM(w_up.shape[1:], bf),
            pltpu.VMEM(w_down.shape[1:], bf),
            pltpu.VMEM((both, (half + TABLE) // 2), bf),
            pltpu.VMEM((both, half // 2), bf),
            pltpu.VMEM((both, half // 2), bf),
            pltpu.VMEM((chips * both, hidden_count), jnp.float32),
            pltpu.VMEM((chips * both, hidden_count), jnp.float32),
        ]
        + gather_shapes * 2
        + scatter_shapes * 4
        + [
            pltpu.SemaphoreType.DMA((3,)),
            pltpu.SemaphoreType.DMA((8,)),
            pltpu.SemaphoreType.DMA((8,)),
            pltpu.SemaphoreType.DMA((6 * chips,)),
            pltpu.SemaphoreType.DMA((6 * chips,)),
        ],
        compiler_params=pltpu.CompilerParams(
            collective_id=0, has_side_effects=True, vmem_limit_bytes=56 * 1024 * 1024
        ),
    )(folded, w_gate, w_up, w_down)


def migrate_kernel(
    peers,
    dest_ref,
    slot_ref,
    length_ref,
    cache_ref,
    arrived_ref,
    meta_ref,
    cache_out,
    cache_in,
    meta_out,
    meta_in,
    cache_send,
    cache_recv,
    meta_send,
    meta_recv,
):
    me = lax.axis_index("ep")
    owned = cache_ref.shape[0]
    per = owned // SPAN
    ahead = [lax.rem(me + o, peers) for o in range(SPAN)]
    behind = [lax.rem(me + peers - o, peers) for o in range(SPAN)]
    barrier = pltpu.get_barrier_semaphore()
    for o in range(1, SPAN):
        pl.semaphore_signal(barrier, inc=1, device_id={"ep": ahead[o]})
        pl.semaphore_signal(barrier, inc=1, device_id={"ep": behind[o]})

    counts = [jnp.int32(0)] * SPAN
    chosen = [[jnp.int32(0)] * per for _ in range(SPAN)]
    for i in range(owned):
        gap = dest_ref[i] - me
        gap = jnp.where(gap < 0, gap + peers, gap)
        for o in range(SPAN):
            here = gap == o
            for k in range(per):
                chosen[o][k] = jnp.where(here & (counts[o] == k), i, chosen[o][k])
            counts[o] = counts[o] + here.astype(jnp.int32)
    lane = lax.broadcasted_iota(jnp.int32, meta_out.shape[1:], 1)

    def describe(o):
        tile = jnp.zeros(meta_out.shape[1:], jnp.int32)
        for k in range(per):
            tile = jnp.where(lane == k, slot_ref[chosen[o][k]], tile)
            tile = jnp.where(lane == per + k, length_ref[chosen[o][k]], tile)
        return tile

    for o in range(1, SPAN):
        for k in range(per):
            cache_out[o - 1, k] = cache_ref[chosen[o][k]]
        meta_out[o - 1] = describe(o)
    pl.semaphore_wait(barrier, 2 * (SPAN - 1))
    copies = []
    for o in range(SPAN - 1, 0, -1):
        for src, dst, send_sem, recv_sem in (
            (cache_out, cache_in, cache_send, cache_recv),
            (meta_out, meta_in, meta_send, meta_recv),
        ):
            copy = pltpu.make_async_remote_copy(
                src_ref=src.at[o - 1],
                dst_ref=dst.at[o - 1],
                send_sem=send_sem.at[o - 1],
                recv_sem=recv_sem.at[o - 1],
                device_id={"ep": ahead[o]},
            )
            copy.start()
            copies.append(copy)
    for k in range(per):
        arrived_ref[k] = cache_ref[chosen[0][k]]
    meta_ref[0] = describe(0)
    for copy in copies:
        copy.wait_recv()
    for o in range(1, SPAN):
        for k in range(per):
            arrived_ref[o * per + k] = cache_in[o - 1, k]
        meta_ref[o] = meta_in[o - 1]
    for copy in copies:
        copy.wait_send()


def migrate(kv_cache, cache_length, dest_device, dest_slot):
    peers = lax.axis_size("ep")
    per = kv_cache.shape[0] // SPAN
    piece = pltpu.VMEM((SPAN - 1, per) + kv_cache.shape[1:], kv_cache.dtype)
    note = pltpu.VMEM((SPAN - 1, 8, 128), jnp.int32)
    smem = pl.BlockSpec(memory_space=pltpu.SMEM)
    vmem = pl.BlockSpec(memory_space=pltpu.VMEM)
    arrived, meta = pl.pallas_call(
        functools.partial(migrate_kernel, peers),
        out_shape=(
            jax.ShapeDtypeStruct(kv_cache.shape, kv_cache.dtype),
            jax.ShapeDtypeStruct((SPAN, 8, 128), jnp.int32),
        ),
        in_specs=[smem, smem, smem, vmem],
        out_specs=(vmem, vmem),
        scratch_shapes=[piece, piece, note, note]
        + [pltpu.SemaphoreType.DMA((SPAN - 1,))] * 4,
        compiler_params=pltpu.CompilerParams(
            collective_id=1, has_side_effects=True, vmem_limit_bytes=16 * 1024 * 1024
        ),
    )(dest_device, dest_slot, cache_length, kv_cache)
    return arrived, meta[:, 0, :per], meta[:, 0, per : 2 * per]


def apply_rows(selector, values):
    return jnp.dot(selector, values, preferred_element_type=jnp.float32).astype(jnp.bfloat16)


def shards(
    kv_cache,
    cache_length,
    dest_device,
    dest_slot,
    query_rows,
    new_kv,
    resid_rows,
    norm_gain,
    route_ids,
    route_weight,
    w_gate,
    w_up,
    w_down,
):
    device_count = lax.axis_size("ep")
    owned_count = kv_cache.shape[0]
    incoming, arrived_slot, arrived_length = migrate(
        kv_cache, cache_length, dest_device, dest_slot
    )
    incoming = incoming.reshape(owned_count, -1)
    slot_range = jnp.arange(owned_count, dtype=jnp.int32)[:, None]
    chooser = arrived_slot.reshape(1, owned_count) == slot_range
    moved_cache = apply_rows(chooser.astype(jnp.bfloat16), incoming).reshape(kv_cache.shape)
    moved_length = jnp.sum(
        chooser.astype(jnp.int32) * arrived_length.reshape(1, owned_count), axis=1
    )
    context = attend(query_rows, new_kv, moved_cache, moved_length)
    summed_state = resid_rows.astype(jnp.float32) + context.astype(jnp.float32)
    inverse = lax.rsqrt(jnp.mean(summed_state * summed_state, axis=1, keepdims=True) + 1e-06)
    normed = (summed_state * inverse * norm_gain.astype(jnp.float32)[None, :]).astype(jnp.bfloat16)
    experts = device_count // 2
    hits = route_ids[:, :, None] == jnp.arange(experts, dtype=jnp.int32)[None, None, :]
    table = jnp.sum(
        jnp.where(hits, route_weight.astype(jnp.float32)[:, :, None], 0.0), axis=1
    ).astype(jnp.bfloat16)
    moe_out = expert_layer(normed, table, w_gate, w_up, w_down)
    return (moved_cache, context, moe_out)


def solution(mesh):
    placed = (
        P(("groups", "ep"), None, None),
        P(("groups", "ep")),
        P(("groups", "ep")),
        P(("groups", "ep")),
        P(("groups", "ep"), None),
        P(("groups", "ep"), None),
        P(("groups", "ep"), None),
        P(),
        P(("groups", "ep"), None),
        P(("groups", "ep"), None),
        P("ep", None, None),
        P("ep", None, None),
        P("ep", None, None),
    )
    return jax.shard_map(
        shards,
        mesh=mesh,
        in_specs=placed,
        out_specs=(
            P(("groups", "ep"), None, None),
            P(("groups", "ep"), None),
            P(("groups", "ep"), None),
        ),
        check_vma=False,
    )
```

```python
import functools
import math

import jax
import jax.numpy as jnp
from jax import lax
from jax.experimental import pallas as pl
from jax.experimental.pallas import tpu as pltpu
from jax.sharding import PartitionSpec as P

HEAD_DIM = 128
Q_HEADS = 32
KV_HEADS = 2
TOPK = 8
SPAN = 4
LEN = 32


def attend(query_rows, new_kv, kv_cache, cache_length):
    row_count = query_rows.shape[0]
    group_size = Q_HEADS // KV_HEADS
    score_scale = 1.0 / math.sqrt(HEAD_DIM)
    queries = query_rows.reshape(row_count, KV_HEADS, group_size, HEAD_DIM)
    stored = kv_cache.reshape(row_count, LEN, 2, KV_HEADS, HEAD_DIM)
    fresh = new_kv.reshape(row_count, 2, KV_HEADS, HEAD_DIM)
    scores = (
        jnp.einsum("rgjd,rtgd->rgjt", queries, stored[:, :, 0], preferred_element_type=jnp.float32)
        * score_scale
    )
    own_score = (
        jnp.einsum("rgjd,rgd->rgj", queries, fresh[:, 0], preferred_element_type=jnp.float32)
        * score_scale
    )
    in_range = (jnp.arange(LEN, dtype=jnp.int32)[None, :] < cache_length[:, None])[:, None, None, :]
    masked = jnp.where(in_range, scores, -jnp.inf)
    peak = jnp.maximum(jnp.max(masked, axis=-1), own_score)
    weights = jnp.where(in_range, jnp.exp(scores - peak[..., None]), 0.0)
    own_weight = jnp.exp(own_score - peak)
    denominator = jnp.sum(weights, axis=-1) + own_weight
    probs = (weights / denominator[..., None]).astype(jnp.bfloat16)
    own_prob = (own_weight / denominator).astype(jnp.bfloat16)
    context = jnp.einsum(
        "rgjt,rtgd->rgjd", probs, stored[:, :, 1], preferred_element_type=jnp.float32
    )
    context = (
        context
        + own_prob.astype(jnp.float32)[..., None] * fresh[:, 1].astype(jnp.float32)[:, :, None, :]
    )
    return context.reshape(row_count, Q_HEADS * HEAD_DIM).astype(jnp.bfloat16)


TABLE = 256


def bit_orders(bits):
    down = list(reversed(range(bits)))
    swapped = down[:-2] + [down[-1], down[-2]]
    early = [0, 1] + list(reversed(range(2, bits)))
    return (down, swapped, early)


def relative(order, place):
    return sum(1 << order[j] for j in range(len(order)) if place >> j & 1)


def widths(half):
    tiles = half // 128
    first = (tiles - 2) // 3
    second = (tiles - first) // 2
    gather = (first * 128, second * 128, (tiles - first - second) * 128)
    third = tiles // 3
    rest = (tiles - third) // 2
    scatter = (third * 128, rest * 128, (tiles - third - rest) * 128)
    return gather, scatter


def fold_wide(value):
    cut = value.shape[1] // 2
    return jnp.concatenate([value[:, :cut], value[:, cut:]], axis=0)


def unfold_wide(value):
    cut = value.shape[0] // 2
    return jnp.concatenate([value[:cut], value[cut:]], axis=1)


def expert_kernel(
    bits,
    folded_ref,
    gate_hbm,
    up_hbm,
    down_hbm,
    out_ref,
    gate_ref,
    up_ref,
    down_ref,
    stage,
    last_send,
    last_recv,
    gate_sum,
    up_sum,
    g0,
    g1,
    g2,
    o0,
    o1,
    o2,
    s0,
    s1,
    s2,
    d0,
    d1,
    d2,
    a0,
    a1,
    a2,
    e0,
    e1,
    e2,
    load_sem,
    pair_send,
    pair_recv,
    step_send,
    step_recv,
):
    chips = 1 << bits
    width = down_ref.shape[1]
    half = width // 2
    gather, scatter = widths(half)
    orders = bit_orders(bits)
    held, other = (g0, g1, g2), (o0, o1, o2)
    given, taken, total, landed = (s0, s1, s2), (d0, d1, d2), (a0, a1, a2), (e0, e1, e2)
    me = lax.axis_index("ep")
    chip = me // 2
    core = me % 2
    mate = me + 1 - 2 * core
    far = []
    for bit in range(bits):
        own_bit = (chip // (1 << bit)) % 2
        far.append(me + (1 - 2 * own_bit) * (2 << bit))

    loads = []
    for k, (src, dst) in enumerate(
        ((gate_hbm, gate_ref), (up_hbm, up_ref), (down_hbm, down_ref))
    ):
        load = pltpu.make_async_copy(src.at[0], dst, load_sem.at[k])
        load.start()
        loads.append(load)

    barrier = pltpu.get_barrier_semaphore()
    for target in [mate] + far:
        pl.semaphore_signal(barrier, inc=1, device_id={"ep": target})
    pl.semaphore_wait(barrier, 1 + bits)

    def send(src, dst, send_sem, recv_sem, target):
        copy = pltpu.make_async_remote_copy(
            src_ref=src,
            dst_ref=dst,
            send_sem=send_sem,
            recv_sem=recv_sem,
            device_id={"ep": target},
        )
        copy.start()
        return copy

    sent = []
    first = send(folded_ref.at[1 - core], stage, pair_send.at[0], pair_recv.at[0], mate)
    sent.append(first)
    mine = unfold_wide(folded_ref[core].astype(jnp.float32))
    first.wait_recv()
    theirs = unfold_wide(stage[...].astype(jnp.float32))
    block = jnp.where(
        core == 0,
        jnp.concatenate([mine, theirs], axis=0),
        jnp.concatenate([theirs, mine], axis=0),
    ).astype(jnp.bfloat16)
    starts = (0, gather[0], gather[0] + gather[1])
    held[0][0] = jnp.concatenate(
        [block[:, : gather[0]], block[:, half:]], axis=1
    )
    for c in (1, 2):
        held[c][0] = block[:, starts[c] : starts[c] + gather[c]]

    by_depth = sorted(range(chips), key=lambda p: (p.bit_count(), p))
    hops = {}
    for p in by_depth:
        for c in range(3):
            if p > 0:
                hops[c, p].wait_recv()
            for i in range(p.bit_length(), bits):
                to = p + (1 << i)
                hops[c, to] = send(
                    held[c].at[p],
                    held[c].at[to],
                    step_send.at[c * chips + to],
                    step_recv.at[c * chips + to],
                    far[orders[c][i]],
                )
                sent.append(hops[c, to])
    loads[0].wait()
    loads[1].wait()

    def operand(buffer, c):
        place = {relative(orders[c], p): p for p in range(chips)}
        return jnp.concatenate([buffer[place[r]] for r in range(chips)], axis=0)

    def accumulate(rows, c, side, fresh):
        base = pl.multiple_of(side * half + starts[c], 128)
        left = rows[:, : gather[c]]
        g = jnp.dot(
            left, gate_ref[pl.ds(base, gather[c]), :], preferred_element_type=jnp.float32
        )
        u = jnp.dot(
            left, up_ref[pl.ds(base, gather[c]), :], preferred_element_type=jnp.float32
        )
        if fresh:
            gate_sum[...] = g
            up_sum[...] = u
        else:
            gate_sum[...] += g
            up_sum[...] += u

    swaps = []
    share = None
    for c in range(3):
        swap = send(held[c], other[c], pair_send.at[1 + c], pair_recv.at[1 + c], mate)
        swaps.append(swap)
        sent.append(swap)
        rows = operand(held[c], c)
        if c == 0:
            tables = rows[:, gather[0] :].astype(jnp.float32)
            lane = lax.broadcasted_iota(jnp.int32, tables.shape, 1)
            share = jnp.sum(jnp.where(lane == chip, tables, 0.0), axis=1, keepdims=True)
        accumulate(rows, c, core, c == 0)
    for c in range(3):
        swaps[c].wait_recv()
        accumulate(operand(other[c], c), c, 1 - core, False)

    gate = gate_sum[...]
    hidden = (gate * jax.nn.sigmoid(gate) * up_sum[...]).astype(jnp.bfloat16)
    loads[2].wait()
    begins = (0, scatter[0], scatter[0] + scatter[1])

    def down(c, side):
        base = pl.multiple_of(side * half + begins[c], 128)
        return (
            jnp.dot(
                hidden, down_ref[:, pl.ds(base, scatter[c])], preferred_element_type=jnp.float32
            )
            * share
        )

    trades = []
    for c in range(3):
        value = down(c, 1 - core).astype(jnp.bfloat16)
        for p in range(chips):
            r = relative(orders[c], p)
            given[c][p] = value[16 * r : 16 * r + 16]
        trade = send(given[c], taken[c], pair_send.at[4 + c], pair_recv.at[4 + c], mate)
        trades.append(trade)
        sent.append(trade)
    base_sem = 3 * chips
    backs = {}

    def back(c, p):
        i = p.bit_length() - 1
        backs[c, p] = send(
            total[c].at[p],
            landed[c].at[p],
            step_send.at[base_sem + c * chips + p],
            step_recv.at[base_sem + c * chips + p],
            far[orders[c][i]],
        )
        sent.append(backs[c, p])

    def block_of(p, values, c):
        r = relative(orders[c], p)
        return values[16 * r : 16 * r + 16] + taken[c][p].astype(jnp.float32)

    for c in range(3):
        value = down(c, core)
        trades[c].wait_recv()
        for p in reversed(by_depth):
            total[c][p] = block_of(p, value, c).astype(jnp.bfloat16)
            if p >= chips // 2:
                back(c, p)
    ends = []
    for p in reversed(by_depth):
        if p >= chips // 2:
            continue
        for c in range(3):
            value = total[c][p].astype(jnp.float32)
            for i in reversed(range(p.bit_length(), bits)):
                backs[c, p + (1 << i)].wait_recv()
                value = value + landed[c][p + (1 << i)].astype(jnp.float32)
            if p > 0:
                total[c][p] = value.astype(jnp.bfloat16)
                back(c, p)
            else:
                ends.append(value)
    done = jnp.concatenate(ends, axis=1)
    rows = done.shape[0] // 2
    keep = jnp.where(core == 0, done[:rows], done[rows:])
    pass_on = jnp.where(core == 0, done[rows:], done[:rows])
    last_send[...] = fold_wide(pass_on).astype(jnp.bfloat16)
    final = send(last_send, last_recv, pair_send.at[7], pair_recv.at[7], mate)
    sent.append(final)
    final.wait_recv()
    got = unfold_wide(last_recv[...].astype(jnp.float32))
    out_ref[...] = jnp.where(
        core == 0,
        jnp.concatenate([keep, got], axis=1),
        jnp.concatenate([got, keep], axis=1),
    ).astype(out_ref.dtype)
    for copy in sent:
        copy.wait_send()


def expert_layer(normed, table, w_gate, w_up, w_down):
    devices = lax.axis_size("ep")
    bits = (devices // 2).bit_length() - 1
    chips = 1 << bits
    rows, width = normed.shape
    half = width // 2
    gather, scatter = widths(half)
    padded = jnp.pad(table, ((0, 0), (0, TABLE - table.shape[1])))
    folded = jnp.stack(
        [
            fold_wide(jnp.concatenate([normed[:, h * half : (h + 1) * half], padded], axis=1))
            for h in (0, 1)
        ]
    )
    both = 2 * rows
    bf = jnp.bfloat16
    gather_shapes = [
        pltpu.VMEM((chips, both, gather[c] + (TABLE if c == 0 else 0)), bf) for c in range(3)
    ]
    scatter_shapes = [pltpu.VMEM((chips, both, scatter[c]), bf) for c in range(3)]
    hidden_count = w_gate.shape[2]
    return pl.pallas_call(
        functools.partial(expert_kernel, bits),
        out_shape=jax.ShapeDtypeStruct((rows, width), bf),
        in_specs=[pl.BlockSpec(memory_space=pltpu.VMEM)]
        + [pl.BlockSpec(memory_space=pl.ANY)] * 3,
        out_specs=pl.BlockSpec(memory_space=pltpu.VMEM),
        scratch_shapes=[
            pltpu.VMEM(w_gate.shape[1:], bf),
            pltpu.VMEM(w_up.shape[1:], bf),
            pltpu.VMEM(w_down.shape[1:], bf),
            pltpu.VMEM((both, (half + TABLE) // 2), bf),
            pltpu.VMEM((both, half // 2), bf),
            pltpu.VMEM((both, half // 2), bf),
            pltpu.VMEM((chips * both, hidden_count), jnp.float32),
            pltpu.VMEM((chips * both, hidden_count), jnp.float32),
        ]
        + gather_shapes * 2
        + scatter_shapes * 4
        + [
            pltpu.SemaphoreType.DMA((3,)),
            pltpu.SemaphoreType.DMA((8,)),
            pltpu.SemaphoreType.DMA((8,)),
            pltpu.SemaphoreType.DMA((6 * chips,)),
            pltpu.SemaphoreType.DMA((6 * chips,)),
        ],
        compiler_params=pltpu.CompilerParams(
            collective_id=0, has_side_effects=True, vmem_limit_bytes=56 * 1024 * 1024
        ),
    )(folded, w_gate, w_up, w_down)


def migrate_kernel(
    peers,
    dest_hbm,
    slot_hbm,
    length_hbm,
    cache_ref,
    arrived_ref,
    meta_ref,
    cache_out,
    cache_in,
    meta_out,
    meta_in,
    cache_send,
    cache_recv,
    meta_send,
    meta_recv,
    dest_ref,
    slot_ref,
    length_ref,
    load_sem,
):
    loads = []
    for n, (src, dst) in enumerate(
        ((dest_hbm, dest_ref), (slot_hbm, slot_ref), (length_hbm, length_ref))
    ):
        load = pltpu.make_async_copy(src, dst, load_sem.at[n])
        load.start()
        loads.append(load)
    me = lax.axis_index("ep")
    owned = cache_ref.shape[0]
    per = owned // SPAN
    ahead = [lax.rem(me + o, peers) for o in range(SPAN)]
    behind = [lax.rem(me + peers - o, peers) for o in range(SPAN)]
    barrier = pltpu.get_barrier_semaphore()
    for o in range(1, SPAN):
        pl.semaphore_signal(barrier, inc=1, device_id={"ep": ahead[o]})
        pl.semaphore_signal(barrier, inc=1, device_id={"ep": behind[o]})

    for load in loads:
        load.wait()
    counts = [jnp.int32(0)] * SPAN
    chosen = [[jnp.int32(0)] * per for _ in range(SPAN)]
    for i in range(owned):
        gap = dest_ref[i] - me
        gap = jnp.where(gap < 0, gap + peers, gap)
        for o in range(SPAN):
            here = gap == o
            for k in range(per):
                chosen[o][k] = jnp.where(here & (counts[o] == k), i, chosen[o][k])
            counts[o] = counts[o] + here.astype(jnp.int32)
    lane = lax.broadcasted_iota(jnp.int32, meta_out.shape[1:], 1)

    def describe(o):
        tile = jnp.zeros(meta_out.shape[1:], jnp.int32)
        for k in range(per):
            tile = jnp.where(lane == k, slot_ref[chosen[o][k]], tile)
            tile = jnp.where(lane == per + k, length_ref[chosen[o][k]], tile)
        return tile

    for o in range(1, SPAN):
        for k in range(per):
            cache_out[o - 1, k] = cache_ref[chosen[o][k]]
        meta_out[o - 1] = describe(o)
    pl.semaphore_wait(barrier, 2 * (SPAN - 1))
    copies = []
    for o in range(SPAN - 1, 0, -1):
        for src, dst, send_sem, recv_sem in (
            (cache_out, cache_in, cache_send, cache_recv),
            (meta_out, meta_in, meta_send, meta_recv),
        ):
            copy = pltpu.make_async_remote_copy(
                src_ref=src.at[o - 1],
                dst_ref=dst.at[o - 1],
                send_sem=send_sem.at[o - 1],
                recv_sem=recv_sem.at[o - 1],
                device_id={"ep": ahead[o]},
            )
            copy.start()
            copies.append(copy)
    for k in range(per):
        arrived_ref[k] = cache_ref[chosen[0][k]]
    meta_ref[0] = describe(0)
    for copy in copies:
        copy.wait_recv()
    for o in range(1, SPAN):
        for k in range(per):
            arrived_ref[o * per + k] = cache_in[o - 1, k]
        meta_ref[o] = meta_in[o - 1]
    for copy in copies:
        copy.wait_send()


def migrate(kv_cache, cache_length, dest_device, dest_slot):
    peers = lax.axis_size("ep")
    per = kv_cache.shape[0] // SPAN
    piece = pltpu.VMEM((SPAN - 1, per) + kv_cache.shape[1:], kv_cache.dtype)
    note = pltpu.VMEM((SPAN - 1, 8, 128), jnp.int32)
    hbm = pl.BlockSpec(memory_space=pl.ANY)
    index = pltpu.SMEM((kv_cache.shape[0],), jnp.int32)
    vmem = pl.BlockSpec(memory_space=pltpu.VMEM)
    arrived, meta = pl.pallas_call(
        functools.partial(migrate_kernel, peers),
        out_shape=(
            jax.ShapeDtypeStruct(kv_cache.shape, kv_cache.dtype),
            jax.ShapeDtypeStruct((SPAN, 8, 128), jnp.int32),
        ),
        in_specs=[hbm, hbm, hbm, vmem],
        out_specs=(vmem, vmem),
        scratch_shapes=[piece, piece, note, note]
        + [pltpu.SemaphoreType.DMA((SPAN - 1,))] * 4
        + [index] * 3
        + [pltpu.SemaphoreType.DMA((3,))],
        compiler_params=pltpu.CompilerParams(
            collective_id=1, has_side_effects=True, vmem_limit_bytes=16 * 1024 * 1024
        ),
    )(dest_device, dest_slot, cache_length, kv_cache)
    return arrived, meta[:, 0, :per], meta[:, 0, per : 2 * per]


def apply_rows(selector, values):
    return jnp.dot(selector, values, preferred_element_type=jnp.float32).astype(jnp.bfloat16)


def shards(
    kv_cache,
    cache_length,
    dest_device,
    dest_slot,
    query_rows,
    new_kv,
    resid_rows,
    norm_gain,
    route_ids,
    route_weight,
    w_gate,
    w_up,
    w_down,
):
    device_count = lax.axis_size("ep")
    owned_count = kv_cache.shape[0]
    incoming, arrived_slot, arrived_length = migrate(
        kv_cache, cache_length, dest_device, dest_slot
    )
    incoming = incoming.reshape(owned_count, -1)
    slot_range = jnp.arange(owned_count, dtype=jnp.int32)[:, None]
    chooser = arrived_slot.reshape(1, owned_count) == slot_range
    moved_cache = apply_rows(chooser.astype(jnp.bfloat16), incoming).reshape(kv_cache.shape)
    moved_length = jnp.sum(
        chooser.astype(jnp.int32) * arrived_length.reshape(1, owned_count), axis=1
    )
    context = attend(query_rows, new_kv, moved_cache, moved_length)
    summed_state = resid_rows.astype(jnp.float32) + context.astype(jnp.float32)
    inverse = lax.rsqrt(jnp.mean(summed_state * summed_state, axis=1, keepdims=True) + 1e-06)
    normed = (summed_state * inverse * norm_gain.astype(jnp.float32)[None, :]).astype(jnp.bfloat16)
    experts = device_count // 2
    hits = route_ids[:, :, None] == jnp.arange(experts, dtype=jnp.int32)[None, None, :]
    table = jnp.sum(
        jnp.where(hits, route_weight.astype(jnp.float32)[:, :, None], 0.0), axis=1
    ).astype(jnp.bfloat16)
    moe_out = expert_layer(normed, table, w_gate, w_up, w_down)
    return (moved_cache, context, moe_out)


def solution(mesh):
    placed = (
        P(("groups", "ep"), None, None),
        P(("groups", "ep")),
        P(("groups", "ep")),
        P(("groups", "ep")),
        P(("groups", "ep"), None),
        P(("groups", "ep"), None),
        P(("groups", "ep"), None),
        P(),
        P(("groups", "ep"), None),
        P(("groups", "ep"), None),
        P("ep", None, None),
        P("ep", None, None),
        P("ep", None, None),
    )
    return jax.shard_map(
        shards,
        mesh=mesh,
        in_specs=placed,
        out_specs=(
            P(("groups", "ep"), None, None),
            P(("groups", "ep"), None),
            P(("groups", "ep"), None),
        ),
        check_vma=False,
    )
```
